256 devices in a mesh: section: 8 (over z), expert: 32 (over y, x, core).
Axes of the slice: x: 4, y: 4, z: 8, core: 2. Of those that a mesh axis runs over, the one named last changes fastest.
Arguments:
- fwd_input: bfloat16 [8, 3072, 7168], P('section', 'expert'), may hold values from -6 to 6
- saved_input: bfloat16 [8, 3072, 7168], P('section', 'expert'), may hold values from -6 to 6
- out_cotangent: bfloat16 [8, 3072, 7168], P('section', 'expert'), may hold values from -6 to 6
- fwd_routes: int32 [8, 3072, 8], P('section', 'expert'), may hold values from 0 to 255, as said below
- bwd_routes: int32 [8, 3072, 8], P('section', 'expert'), may hold values from 0 to 255, as said below
- fwd_scores: float32 [8, 3072, 8], P('section', 'expert'), may hold values from -6 to 6
- bwd_scores: float32 [8, 3072, 8], P('section', 'expert'), may hold values from -6 to 6
- norm_gain: float32 [8, 7168], P('section'), may hold values from 0.1 to 1.9
- gate_proj: bfloat16 [8, 32, 7168, 128], P('section', 'expert'), may hold values from -0.0625 to 0.0625
- up_proj: bfloat16 [8, 32, 7168, 128], P('section', 'expert'), may hold values from -0.0625 to 0.0625
- down_proj: bfloat16 [8, 32, 128, 7168], P('section', 'expert'), may hold values from -0.1875 to 0.1875
Outputs:
- fwd_handoff: bfloat16 [8, 3072, 7168], P('section', 'expert')
- grad_handoff: bfloat16 [8, 3072, 7168], P('section', 'expert')
- score_grads: float32 [8, 3072, 8], P('section', 'expert')
The draws below stay inside these ranges and needn't reach their ends.
Inputs may be any that keep to these rules, and one draw needn't show every extreme that they name: `fwd_routes`: each row names 8 different experts. Among the rows of one device, no expert below 4 is named by more than 8 rows, and in every section one expert below 4 is named by exactly 8 rows of every device. `bwd_routes`: as for fwd_routes.
All inputs are finite; a program needn't handle non-finite values.
Results may differ from the reference program's by a relative error of at most 0.017.
Values may be sent and summed in bfloat16 or wider, within the bound.
No kernel may reach another device: no remote copies, remote signals or barrier semaphores. Data moves between devices by JAX's collectives and lax.ppermute only.
A program may use at most 128 MiB of HBM per device.

```python
import jax
import jax.numpy as jnp
from jax import lax

D = 7168
EXPERTS = 256
TOPK = 8
FE = 1024
GROUP = 8
CAP = 8
ROWS = 96
HID = 128
WINDOW = 4
SLICES = 32
TOKENS = 3072
SECTIONS = 8
N_EXPERT = 32


def route_draw(key):
    blocks = N_EXPERT
    window = N_EXPERT // GROUP
    keys = jax.random.split(key, 5)
    counts = jax.random.randint(keys[0], (SECTIONS, blocks, window), 0, CAP * 3 // 4)
    hottest = jax.random.randint(keys[1], (SECTIONS, 1, 1), 0, window)
    expert_ids = jnp.arange(window, dtype=jnp.int32)[None, None, :]
    counts = jnp.where(expert_ids == hottest, CAP, counts)
    order_keys = jax.random.randint(keys[2], (SECTIONS, blocks, window, ROWS), 0, 65536) * ROWS + jnp.arange(ROWS, dtype=jnp.int32)
    ranks = jnp.argsort(jnp.argsort(order_keys, axis=-1), axis=-1)
    naming = jnp.transpose(ranks < counts[..., None], (0, 1, 3, 2))
    all_ids = jnp.arange(EXPERTS, dtype=jnp.int32)
    random_part = jax.random.randint(keys[3], (SECTIONS, blocks, ROWS, EXPERTS), 0, 65536) * EXPERTS + all_ids
    named_full = jnp.concatenate([naming, jnp.zeros((SECTIONS, blocks, ROWS, EXPERTS - window), jnp.bool_)], axis=-1)
    priority = jnp.where(all_ids < window, jnp.where(named_full, 1073741824 + all_ids, -1 - all_ids), random_part)
    chosen = lax.top_k(priority, TOPK)[1].astype(jnp.int32)
    shuffle = jax.random.randint(keys[4], (SECTIONS, blocks, ROWS, TOPK), 0, 65536) * TOPK + jnp.arange(TOPK, dtype=jnp.int32)
    order = jnp.argsort(shuffle, axis=-1)
    routes = jnp.take_along_axis(chosen, order, axis=-1)
    return routes.reshape(SECTIONS, blocks * ROWS, TOPK).astype(jnp.int32)


def draw_fwd_routes(key, part):
    key = jax.random.fold_in(key, 11)
    return route_draw(key)


def draw_bwd_routes(key, part):
    key = jax.random.fold_in(key, 23)
    return route_draw(key)


def steps_of(stream_key, extent, cuts, least, high):
    factor_of = 1.0
    for dim, blocks in cuts:
        draws = jax.random.uniform(jax.random.fold_in(jax.random.fold_in(stream_key, 6), dim), (blocks,), jnp.float32, least / len(cuts), high / len(cuts))
        factor_of = factor_of * jnp.repeat(jnp.exp(draws), extent[dim] // blocks).reshape((-1,) + (1,) * (len(extent) - 1 - dim))
    return factor_of


def centred(stream_key, shape, scale, bound, shards=(), held_as=jnp.bfloat16):
    array = scale * jax.random.normal(stream_key, shape, jnp.float32)
    if shards:
        array = array * steps_of(stream_key, shape, shards, -0.22, 0.18)
    return jnp.clip(array, -bound, bound).astype(held_as)


def setup_inputs(seed: int = 0) -> dict:
    key_of = jax.random.split(jax.random.key(seed), 12)
    return {
        "fwd_input": centred(key_of[0], (SECTIONS, TOKENS, D), 1.0, 6.0, ((0, 8), (1, 32))),
        "saved_input": centred(key_of[1], (SECTIONS, TOKENS, D), 1.0, 6.0, ((0, 8), (1, 32))),
        "out_cotangent": centred(key_of[2], (SECTIONS, TOKENS, D), 1.0, 6.0, ((0, 8), (1, 32))),
        "fwd_routes": draw_fwd_routes(jax.random.fold_in(key_of[11], 71), 0),
        "bwd_routes": draw_bwd_routes(jax.random.fold_in(key_of[11], 71), 0),
        "fwd_scores": centred(key_of[5], (SECTIONS, TOKENS, TOPK), 2.0, 6.0, ((0, 8), (1, 32)), jnp.float32),
        "bwd_scores": centred(key_of[6], (SECTIONS, TOKENS, TOPK), 2.0, 6.0, ((0, 8), (1, 32)), jnp.float32),
        "norm_gain": jnp.clip(1.0 + 0.18 * jax.random.normal(key_of[7], (SECTIONS, D), jnp.float32), 0.1, 1.9),
        "gate_proj": centred(key_of[8], (SECTIONS, SLICES, D, HID), D ** -0.5, 0.0625, ((0, 8), (1, 32))),
        "up_proj": centred(key_of[9], (SECTIONS, SLICES, D, HID), D ** -0.5, 0.0625, ((0, 8), (1, 32))),
        "down_proj": centred(key_of[10], (SECTIONS, SLICES, HID, D), FE ** -0.5, 0.1875, ((0, 8), (1, 32))),
    }


EPSILON = 1e-06
ROUTE_SCALE = 2.5

def normalize(values, gain_row):
    inverse = lax.rsqrt(lax.optimization_barrier(jnp.mean(values * values, axis=-1, keepdims=True)) + EPSILON)
    return (values * inverse * gain_row, inverse)

def route_tables(routes, scores, window, capacity):
    affinity = jax.nn.sigmoid(scores)
    aff_total = lax.optimization_barrier(jnp.sum(affinity, axis=-1, keepdims=True))
    gate_vals = ROUTE_SCALE * affinity / aff_total
    expert_ids = jnp.arange(window, dtype=jnp.int32)
    matches = (routes[:, :, None] == expert_ids[None, None, :]).astype(jnp.float32)
    naming = lax.optimization_barrier(jnp.sum(matches, axis=1))
    earlier = jnp.cumsum(naming, axis=0) - naming
    slot_ids = jnp.arange(capacity, dtype=jnp.float32)
    table = naming.T[:, None, :] * (earlier.T[:, None, :] == slot_ids[None, :, None]).astype(jnp.float32)
    route_weight = lax.optimization_barrier(jnp.sum(matches * gate_vals[:, :, None], axis=1))
    mixing = table * route_weight.T[:, None, :]
    return (affinity, aff_total, gate_vals, matches, table, mixing)

def slice_forward(inputs, w_gate, w_up, w_down):
    pre_gate = jnp.dot(inputs, w_gate, preferred_element_type=jnp.float32)
    pre_up = jnp.dot(inputs, w_up, preferred_element_type=jnp.float32)
    hidden = (pre_gate * jax.nn.sigmoid(pre_gate) * pre_up).astype(jnp.bfloat16)
    return jnp.dot(hidden, w_down, preferred_element_type=jnp.float32).astype(jnp.bfloat16)

def slice_backward(inputs, cotangent, w_gate, w_up, w_down):
    pre_gate = jnp.dot(inputs, w_gate, preferred_element_type=jnp.float32)
    pre_up = jnp.dot(inputs, w_up, preferred_element_type=jnp.float32)
    gate_sig = jax.nn.sigmoid(pre_gate)
    active = pre_gate * gate_sig
    hidden = (active * pre_up).astype(jnp.bfloat16)
    partial_value = jnp.dot(hidden, w_down, preferred_element_type=jnp.float32).astype(jnp.bfloat16)
    d_hidden = jnp.dot(cotangent, w_down.T, preferred_element_type=jnp.float32)
    d_gate = (d_hidden * pre_up * gate_sig * (1.0 + pre_gate * (1.0 - gate_sig))).astype(jnp.bfloat16)
    d_up = (d_hidden * active).astype(jnp.bfloat16)
    d_input = (jnp.dot(d_gate, w_gate.T, preferred_element_type=jnp.float32) + jnp.dot(d_up, w_up.T, preferred_element_type=jnp.float32)).astype(jnp.bfloat16)
    return (d_input, partial_value)

def gather_slots(table, normed):
    return jnp.einsum('wcr,rd->wcd', table, normed.astype(jnp.float32)).astype(jnp.bfloat16)

def reference(fwd_input, saved_input, out_cotangent, fwd_routes, bwd_routes, fwd_scores, bwd_scores, norm_gain, gate_proj, up_proj, down_proj):
    highest = lax.Precision.HIGHEST
    outs_fwd = []
    outs_bwd = []
    outs_score = []
    for layer_index in range(SECTIONS):
        gain_row = norm_gain[layer_index]
        x_fwd = fwd_input[layer_index].astype(jnp.float32)
        x_bwd = saved_input[layer_index].astype(jnp.float32)
        cot_rows = out_cotangent[layer_index]
        normed_f = normalize(x_fwd, gain_row)[0].astype(jnp.bfloat16)
        normed_b, inverse_b = normalize(x_bwd, gain_row)
        normed_b = normed_b.astype(jnp.bfloat16)
        tabs_f = []
        tabs_b = []
        slots_f = []
        slots_b = []
        slots_c = []
        for block in range(N_EXPERT):
            start_row = block * ROWS
            tab_f = route_tables(fwd_routes[layer_index, start_row:start_row + ROWS], fwd_scores[layer_index, start_row:start_row + ROWS], WINDOW, CAP)
            tab_b = route_tables(bwd_routes[layer_index, start_row:start_row + ROWS], bwd_scores[layer_index, start_row:start_row + ROWS], WINDOW, CAP)
            tabs_f.append(tab_f)
            tabs_b.append(tab_b)
            slots_f.append(gather_slots(tab_f[4], normed_f[start_row:start_row + ROWS]))
            slots_b.append(gather_slots(tab_b[4], normed_b[start_row:start_row + ROWS]))
            slots_c.append(gather_slots(tab_b[4], cot_rows[start_row:start_row + ROWS]))
        stack_f = jnp.stack(slots_f, axis=1)
        stack_b = jnp.stack(slots_b, axis=1)
        stack_c = jnp.stack(slots_c, axis=1)
        expert_f = []
        expert_dn = []
        expert_dot = []
        for expert in range(WINDOW):
            inputs_f = stack_f[expert].reshape(N_EXPERT * CAP, D)
            inputs_b = stack_b[expert].reshape(N_EXPERT * CAP, D)
            cot_in = stack_c[expert].reshape(N_EXPERT * CAP, D)
            total_f = jnp.zeros((N_EXPERT * CAP, D), jnp.float32)
            total_dn = jnp.zeros((N_EXPERT * CAP, D), jnp.float32)
            total_part = jnp.zeros((N_EXPERT * CAP, D), jnp.float32)
            for member in range(GROUP):
                index = expert * GROUP + member
                w_gate = gate_proj[layer_index, index]
                w_up = up_proj[layer_index, index]
                w_down = down_proj[layer_index, index]
                total_f = total_f + slice_forward(inputs_f, w_gate, w_up, w_down).astype(jnp.float32)
                d_input, partial_value = slice_backward(inputs_b, cot_in, w_gate, w_up, w_down)
                total_dn = total_dn + d_input.astype(jnp.float32)
                total_part = total_part + partial_value.astype(jnp.float32)
            dot_vals = lax.optimization_barrier(jnp.sum(cot_in.astype(jnp.float32) * total_part, axis=-1))
            expert_f.append(total_f.reshape(N_EXPERT, CAP, D))
            expert_dn.append(total_dn.reshape(N_EXPERT, CAP, D))
            expert_dot.append(dot_vals.reshape(N_EXPERT, CAP))
        expert_f = jnp.stack(expert_f, axis=0)
        expert_dn = jnp.stack(expert_dn, axis=0)
        expert_dot = jnp.stack(expert_dot, axis=0)
        layer_rows = []
        grad_rows = []
        score_rows = []
        for block in range(N_EXPERT):
            start_row = block * ROWS
            tab_f = tabs_f[block]
            tab_b = tabs_b[block]
            branch = jnp.einsum('wcr,wcd->rd', tab_f[5], expert_f[:, block], precision=highest)
            layer_rows.append((x_fwd[start_row:start_row + ROWS] + branch).astype(jnp.bfloat16))
            affinity, aff_total, gate_vals, matches, table, mixing = tab_b
            dnormed = jnp.einsum('wcr,wcd->rd', mixing, expert_dn[:, block], precision=highest)
            dgate_expert = jnp.einsum('wcr,wc->rw', table, expert_dot[:, block], precision=highest)
            dgate = lax.optimization_barrier(jnp.sum(matches * dgate_expert[:, None, :], axis=2))
            spread_term = lax.optimization_barrier(jnp.sum(dgate * gate_vals, axis=-1, keepdims=True)) / ROUTE_SCALE
            score_rows.append(affinity * (1.0 - affinity) * (ROUTE_SCALE / aff_total) * (dgate - spread_term))
            x_rows = x_bwd[start_row:start_row + ROWS]
            inv_rows = inverse_b[start_row:start_row + ROWS]
            scaled = dnormed * gain_row
            grad = cot_rows[start_row:start_row + ROWS].astype(jnp.float32) + inv_rows * scaled - x_rows * inv_rows * inv_rows * inv_rows * lax.optimization_barrier(jnp.mean(x_rows * scaled, axis=-1, keepdims=True))
            grad_rows.append(grad.astype(jnp.bfloat16))
        outs_fwd.append(jnp.concatenate(layer_rows, axis=0))
        outs_bwd.append(jnp.concatenate(grad_rows, axis=0))
        outs_score.append(jnp.concatenate(score_rows, axis=0))
    layer_out = jnp.stack(outs_fwd, axis=0)
    layer_grad = jnp.stack(outs_bwd, axis=0)
    score_grads = jnp.stack(outs_score, axis=0)
    return (jnp.roll(layer_out, 1, axis=0), jnp.roll(layer_grad, -1, axis=0), score_grads)
```

```python
import functools

import jax
import jax.numpy as jnp
from jax import lax
from jax.experimental import pallas as pl
from jax.experimental.pallas import tpu as pltpu
from jax.sharding import PartitionSpec as P

GROUP = 8
CAP = 8
CORES = 2
LANES = 128
EPSILON = 1e-06
ROUTE_SCALE = 2.5
VMEM_LIMIT = 24 * 1024 * 1024

bf16 = jnp.bfloat16
f32 = jnp.float32


def params():
    return pltpu.CompilerParams(vmem_limit_bytes=VMEM_LIMIT)


def cost(flops, bytes_accessed):
    return pl.CostEstimate(flops=flops, bytes_accessed=bytes_accessed, transcendentals=0)


def dot(a, b, dims=((1,), (0,)), precision=None):
    return lax.dot_general(a, b, (dims, ((), ())), precision=precision, preferred_element_type=f32)


def exact(a, b, dims=((1,), (0,))):
    return dot(a, b, dims, lax.Precision.HIGHEST)


def sigmoid(v):
    return 1.0 / (1.0 + jnp.exp(-v))


def after(array, *others):
    return lax.optimization_barrier((array,) + others)[0]


def split_dot(weights, rows):
    high = weights.astype(bf16)
    low = (weights - high.astype(f32)).astype(bf16)
    return dot(high, rows) + dot(low, rows)


def slot_expert(slots, rows):
    return lax.broadcasted_iota(jnp.int32, (slots, rows), 0) // CAP


def gate_values(scores):
    affinity = sigmoid(scores)
    total = jnp.sum(affinity, axis=0, keepdims=True)
    return affinity, total, ROUTE_SCALE * affinity / total


def tables(routes, scores, slots):
    topk, rows = routes.shape
    expert = slot_expert(slots, rows)
    _, _, gates = gate_values(scores)
    naming = jnp.zeros((slots, rows), f32)
    weight = jnp.zeros((slots, rows), f32)
    for j in range(topk):
        hit = routes[j : j + 1, :] == expert
        naming = naming + jnp.where(hit, 1.0, 0.0)
        weight = weight + jnp.where(hit, gates[j : j + 1, :], 0.0)
    shape = (rows, rows)
    above = lax.broadcasted_iota(jnp.int32, shape, 0) < lax.broadcasted_iota(jnp.int32, shape, 1)
    earlier = dot(naming.astype(bf16), jnp.where(above, 1.0, 0.0).astype(bf16))
    slot = lax.rem(lax.broadcasted_iota(jnp.int32, (slots, rows), 0), CAP)
    here = earlier == slot.astype(f32)
    table = jnp.where(here, naming, 0.0)
    mixing = jnp.where(here, weight, 0.0)
    shape = (slots, slots)
    to = lax.broadcasted_iota(jnp.int32, shape, 0)
    from_ = lax.broadcasted_iota(jnp.int32, shape, 1)
    lower = (lax.rem(from_, CAP) == 0) & (from_ // CAP < to // CAP)
    before = dot(jnp.where(lower, 1.0, 0.0).astype(bf16), naming.astype(bf16))
    first = jnp.where(before == 0.0, table, 0.0)
    return table, mixing, first


def prep_bwd_kernel(
    steps, routes_ref, scores_ref, x_ref, cot_ref, gain_ref, cb_ref, xs_ref, cs_ref, first_ref,
    table_ref, weights_ref, inverse_ref, take_ref, x_slots_ref, c_slots_ref
):
    step = pl.program_id(0)
    slots = take_ref.shape[0]
    block = x_ref.shape[1]

    @pl.when(step == 0)
    def _():
        table, mixing, first = tables(routes_ref[...], scores_ref[...], slots)
        first_ref[...] = first
        table_ref[...] = table
        weights_ref[...] = exact(table, mixing, ((1,), (1,)))
        take_ref[...] = table.astype(bf16)

    take = take_ref[...]
    lanes = pl.ds(pl.multiple_of(step * block, LANES), block)
    x_slots_ref[:, lanes] = dot(take, x_ref[...])
    c_slots_ref[:, lanes] = dot(take, cot_ref[...])

    @pl.when(step == steps - 1)
    def _():
        x = x_slots_ref[...]
        c = c_slots_ref[...]
        inverse = lax.rsqrt(jnp.mean(x * x, axis=1, keepdims=True) + EPSILON)
        inverse_ref[...] = jnp.broadcast_to(inverse, inverse_ref.shape)
        normed = x * inverse * gain_ref[...]
        xs_ref[...] = x.astype(bf16)
        cs_ref[...] = c.astype(bf16)
        for k in range(slots // CAP):
            part = slice(k * CAP, (k + 1) * CAP)
            both = jnp.concatenate([c[part], normed[part]], axis=0).astype(bf16)
            cb_ref[2 * k * CAP : 2 * (k + 1) * CAP, :] = both


def prep_fwd_kernel(
    steps, routes_ref, scores_ref, x_ref, gain_ref, out_ref, mixing_ref, take_ref,
    x_slots_ref
):
    step = pl.program_id(0)
    slots = take_ref.shape[0]
    block = x_ref.shape[1]

    @pl.when(step == 0)
    def _():
        table, mixing, _ = tables(routes_ref[...], scores_ref[...], slots)
        mixing_ref[...] = mixing
        take_ref[...] = table.astype(bf16)

    lanes = pl.ds(pl.multiple_of(step * block, LANES), block)
    x_slots_ref[:, lanes] = dot(take_ref[...], x_ref[...])

    @pl.when(step == steps - 1)
    def _():
        x = x_slots_ref[...]
        inverse = lax.rsqrt(jnp.mean(x * x, axis=1, keepdims=True) + EPSILON)
        out_ref[...] = (x * inverse * gain_ref[...]).astype(bf16)


def vmem():
    return pl.BlockSpec(memory_space=pltpu.VMEM)


def whole(shape):
    return pl.BlockSpec(shape, lambda *_: (0,) * len(shape))


def across(rows, block):
    return pl.BlockSpec((rows, block), lambda i: (0, i))


def prep_bwd(routes, scores, x, cot, gain, window):
    rows, width = x.shape
    slots = window * CAP
    steps = 4
    block = width // steps
    shapes = [
        ((2 * slots, width), bf16),
        ((slots, width), bf16),
        ((slots, width), bf16),
        ((slots, rows), f32),
        ((slots, rows), f32),
        ((slots, slots), f32),
        ((slots, LANES), f32),
    ]
    return pl.pallas_call(
        functools.partial(prep_bwd_kernel, steps),
        out_shape=[jax.ShapeDtypeStruct(*s) for s in shapes],
        grid=(steps,),
        in_specs=[whole(routes.shape), whole(scores.shape)]
        + [across(rows, block)] * 2
        + [whole(gain.shape)],
        out_specs=[whole(s[0]) for s in shapes],
        scratch_shapes=[
            pltpu.VMEM((slots, rows), bf16),
            pltpu.VMEM((slots, width), f32),
            pltpu.VMEM((slots, width), f32),
        ],
        compiler_params=params(),
        cost_estimate=cost(4 * slots * rows * width, 8 * rows * width),
        name="prep_bwd",
    )(routes, scores, x, cot, gain)


def prep_fwd(routes, scores, x, gain, window):
    rows, width = x.shape
    slots = window * CAP
    steps = 4
    block = width // steps
    return pl.pallas_call(
        functools.partial(prep_fwd_kernel, steps),
        out_shape=[
            jax.ShapeDtypeStruct((slots, width), bf16),
            jax.ShapeDtypeStruct((slots, rows), f32),
        ],
        grid=(steps,),
        in_specs=[whole(routes.shape), whole(scores.shape)]
        + [across(rows, block), whole(gain.shape)],
        out_specs=[whole((slots, width)), whole((slots, rows))],
        scratch_shapes=[pltpu.VMEM((slots, rows), bf16), pltpu.VMEM((slots, width), f32)],
        compiler_params=params(),
        cost_estimate=cost(2 * slots * rows * width, 4 * rows * width),
        name="prep_fwd",
    )(routes, scores, x, gain)


def enter_bwd_kernel(steps, chunks, *refs):
    cot_refs, row_refs = refs[:chunks], refs[chunks : 2 * chunks]
    gate_ref, up_ref, down_ref, both_ref, dh_ref = refs[2 * chunks :]
    step = pl.program_id(0)
    weights = jnp.concatenate([gate_ref[...], up_ref[...]], axis=1)
    both = dot(jnp.concatenate([r[...] for r in row_refs], axis=0), weights)
    cots = jnp.concatenate([r[...] for r in cot_refs], axis=0)
    dh = dot(cots, down_ref[...], ((1,), (1,)))

    @pl.when(step == 0)
    def _():
        both_ref[...] = both
        dh_ref[...] = dh

    @pl.when(step > 0)
    def _():
        both_ref[...] += both
        dh_ref[...] += dh


def enter_bwd(cots, inputs, gate, up, down):
    width, hidden = gate.shape
    steps = 4
    block = width // steps
    part = 32
    total = len(cots) * part
    pick = lambda k: pl.BlockSpec((part, block), lambda i: (k, i))
    return pl.pallas_call(
        functools.partial(enter_bwd_kernel, steps, len(cots)),
        out_shape=[
            jax.ShapeDtypeStruct((total, 2 * hidden), f32),
            jax.ShapeDtypeStruct((total, hidden), f32),
        ],
        grid=(steps,),
        in_specs=[pick(k) for _, k in cots + inputs]
        + [pl.BlockSpec((block, hidden), lambda i: (i, 0))] * 2
        + [pl.BlockSpec((hidden, block), lambda i: (0, i))],
        out_specs=[whole((total, 2 * hidden)), whole((total, hidden))],
        compiler_params=params(),
        cost_estimate=cost(6 * total * width * hidden, 4 * total * width + 6 * width * hidden),
        name="enter_bwd",
    )(*[a for a, _ in cots + inputs], gate, up, down)


def leave_bwd_kernel(steps, near_both, near_dh, far_both, far_dh, gate_ref, up_ref, *refs):
    own_ref, peer_ref, da_ref, q_ref = refs
    step = pl.program_id(0)
    hidden = gate_ref.shape[1]
    block = gate_ref.shape[0]

    @pl.when(step == 0)
    def _():
        n, m = near_dh.shape[0] // 2, far_dh.shape[0] // 2

        def joined(a, b):
            return jnp.concatenate([a[:n], b[:m], a[n:], b[m:]], axis=0)

        both = joined(near_both[...], far_both[...])
        dh = joined(near_dh[...], far_dh[...])
        pre_gate = both[:, :hidden]
        pre_up = both[:, hidden:]
        sig = sigmoid(pre_gate)
        active = pre_gate * sig
        h = (active * pre_up).astype(bf16).astype(f32)
        da = dh * pre_up * sig * (1.0 + pre_gate * (1.0 - sig))
        db = dh * active
        da_ref[...] = jnp.concatenate([da, db], axis=1).astype(bf16)
        q = jnp.sum(dh * h, axis=1, keepdims=True)
        q_ref[...] = jnp.broadcast_to(q, q_ref.shape).astype(bf16)

    weights = jnp.concatenate([gate_ref[...], up_ref[...]], axis=1)
    grads = dot(da_ref[...], weights, ((1,), (1,))).astype(bf16)
    lanes = pl.ds(pl.multiple_of(step * block, LANES), block)
    middle = grads.shape[0] // 2
    own_ref[:, lanes] = grads[:middle]
    peer_ref[:, lanes] = grads[middle:]

    @pl.when(step == steps - 1)
    def _():
        own_ref[:, steps * block :] = q_ref[:middle, :]
        peer_ref[:, steps * block :] = q_ref[middle:, :]


def leave_bwd(near, far, gate, up):
    width, hidden = gate.shape
    steps = 4
    block = width // steps
    total = near[1].shape[0] + far[1].shape[0]
    out = jax.ShapeDtypeStruct((total // 2, width + LANES), bf16)
    small = [*near, *far]
    return pl.pallas_call(
        functools.partial(leave_bwd_kernel, steps),
        out_shape=[out, out],
        grid=(steps,),
        in_specs=[whole(a.shape) for a in small]
        + [pl.BlockSpec((block, hidden), lambda i: (i, 0))] * 2,
        out_specs=[whole(out.shape)] * 2,
        scratch_shapes=[pltpu.VMEM((total, 2 * hidden), bf16), pltpu.VMEM((total, LANES), bf16)],
        compiler_params=params(),
        cost_estimate=cost(4 * total * width * hidden, 2 * total * width + 4 * width * hidden),
        name="leave_bwd",
    )(*small, gate, up)


def expert_fwd_kernel(steps, chunks, *refs):
    rows_refs = refs[:chunks]
    gate_ref, up_ref, down_ref, own_ref, peer_ref, both_ref, h_ref = refs[chunks:]
    step = pl.program_id(0)
    hidden = gate_ref.shape[1]
    block = gate_ref.shape[0]

    @pl.when(step < steps)
    def _():
        weights = jnp.concatenate([gate_ref[...], up_ref[...]], axis=1)
        both = dot(jnp.concatenate([r[...] for r in rows_refs], axis=0), weights)

        @pl.when(step == 0)
        def _():
            both_ref[...] = both

        @pl.when(step > 0)
        def _():
            both_ref[...] += both

    @pl.when(step == steps - 1)
    def _():
        pre_gate = both_ref[:, :hidden]
        h_ref[...] = (pre_gate * sigmoid(pre_gate) * both_ref[:, hidden:]).astype(bf16)

    @pl.when(step >= steps)
    def _():
        outs = dot(h_ref[...], down_ref[...]).astype(bf16)
        lanes = pl.ds(pl.multiple_of((step - steps) * block, LANES), block)
        middle = outs.shape[0] // 2
        own_ref[:, lanes] = outs[:middle]
        peer_ref[:, lanes] = outs[middle:]


def expert_fwd(own, peer, gate, up, down):
    width, hidden = gate.shape
    steps = 4
    block = width // steps
    chunks = own + peer
    rows = sum(c.shape[0] for c in own)
    take = lambda i: jnp.minimum(i, steps - 1)
    out = jax.ShapeDtypeStruct((rows, width), bf16)
    return pl.pallas_call(
        functools.partial(expert_fwd_kernel, steps, len(chunks)),
        out_shape=[out, out],
        grid=(2 * steps,),
        in_specs=[pl.BlockSpec((c.shape[0], block), lambda i: (0, take(i))) for c in chunks]
        + [
            pl.BlockSpec((block, hidden), lambda i: (take(i), 0)),
            pl.BlockSpec((block, hidden), lambda i: (take(i), 0)),
            pl.BlockSpec((hidden, block), lambda i: (0, jnp.maximum(i - steps, 0))),
        ],
        out_specs=[whole(out.shape)] * 2,
        scratch_shapes=[
            pltpu.VMEM((2 * rows, 2 * hidden), f32),
            pltpu.VMEM((2 * rows, hidden), bf16),
        ],
        compiler_params=params(),
        cost_estimate=cost(12 * rows * width * hidden, 8 * rows * width + 6 * width * hidden),
        name="expert_fwd",
    )(*chunks, gate, up, down)


def grad_slots_kernel(
    routes_ref, scores_ref, table_ref, weights_ref, inverse_ref, xs_ref, cs_ref, gain_ref, dn_ref,
    grad_ref, score_ref
):
    slots, width = xs_ref.shape
    t = split_dot(weights_ref[...], dn_ref[:, :width]) * gain_ref[...]
    x = xs_ref[...].astype(f32)
    inverse = inverse_ref[:, :1]
    mean = jnp.mean(x * t, axis=1, keepdims=True)
    grad = cs_ref[...].astype(f32) + inverse * t - x * (inverse * inverse * inverse * mean)
    grad_ref[...] = grad.astype(bf16)

    routes = routes_ref[...]
    topk, rows = routes.shape
    spread = table_ref[...] * dn_ref[:, width:].astype(f32)[:, :1]
    expert = slot_expert(slots, rows)
    place = lax.broadcasted_iota(jnp.int32, (topk, rows), 0)
    dgate = jnp.zeros((topk, rows), f32)
    for j in range(topk):
        hit = routes[j : j + 1, :] == expert
        value = jnp.sum(jnp.where(hit, spread, 0.0), axis=0, keepdims=True)
        dgate = jnp.where(place == j, value, dgate)
    affinity, total, gates = gate_values(scores_ref[...])
    term = jnp.sum(dgate * gates, axis=0, keepdims=True) / ROUTE_SCALE
    score_ref[...] = affinity * (1.0 - affinity) * (ROUTE_SCALE / total) * (dgate - term)


def grad_slots(routes, scores, table, weights, inverse, xs, cs, gain, dn):
    slots, width = xs.shape
    return pl.pallas_call(
        grad_slots_kernel,
        out_shape=[
            jax.ShapeDtypeStruct((slots, width), bf16),
            jax.ShapeDtypeStruct(scores.shape, f32),
        ],
        in_specs=[vmem()] * 9,
        out_specs=[vmem()] * 2,
        compiler_params=params(),
        cost_estimate=cost(4 * slots * slots * width, 8 * slots * width),
        name="grad_slots",
    )(routes, scores, table, weights, inverse, xs, cs, gain, dn)


def stacked(refs):
    return jnp.concatenate([r[...].astype(f32) for r in refs], axis=0)


def place_grad_kernel(first_ref, top_ref, bottom_ref, slots_ref, out_ref):
    first = first_ref[...].astype(bf16)
    touched = dot(first, jnp.ones((first.shape[0], LANES), bf16), ((0,), (0,)))[:, :1]
    placed = dot(first, slots_ref[...], ((0,), (0,)))
    out_ref[...] = jnp.where(touched > 0.0, placed, stacked([top_ref, bottom_ref])).astype(bf16)


def place_fwd_kernel(mixing_ref, top_ref, bottom_ref, *refs):
    out_ref = refs[-1]
    mixing = mixing_ref[...]
    high = mixing.astype(bf16)
    low = (mixing - high.astype(f32)).astype(bf16)
    rows = stacked(refs[:-1]).astype(bf16)
    branch = dot(high, rows, ((0,), (0,))) + dot(low, rows, ((0,), (0,)))
    out_ref[...] = (stacked([top_ref, bottom_ref]) + branch).astype(bf16)


def place(kernel, name, table, early, *blocks):
    slots, rows = table.shape
    width = early[0].shape[1]
    steps = 4
    block = width // steps
    return pl.pallas_call(
        kernel,
        out_shape=jax.ShapeDtypeStruct((rows, width), bf16),
        grid=(steps,),
        in_specs=[whole(table.shape)] + [across(b.shape[0], block) for b in [*early, *blocks]],
        out_specs=across(rows, block),
        compiler_params=params(),
        cost_estimate=cost(4 * rows * slots * width, 6 * rows * width),
        name=name,
    )(table, *early, *blocks)


class Net:
    def __init__(self, sections, devices, window):
        self.sections, self.devices = sections, devices
        self.rows = window
        self.columns = devices // window // CORES
        self.row_groups = [
            [self.index(y, x, c) for y in range(self.rows)]
            for x in range(self.columns)
            for c in range(CORES)
        ]

    def index(self, y, x, c):
        return ((y % self.rows) * self.columns + x % self.columns) * CORES + c % CORES

    def pairs(self, dy, dx, dc):
        return [
            (self.index(y, x, c), self.index(y + dy, x + dx, c + dc))
            for y in range(self.rows)
            for x in range(self.columns)
            for c in range(CORES)
        ]

    def move(self, array, dy=0, dx=0, dc=0):
        return lax.ppermute(array, "expert", self.pairs(dy, dx, dc))

    def relay(self, array, by, dy=0):
        if dy == 0:
            pairs = [(s, (s + by) % self.sections) for s in range(self.sections)]
            return lax.ppermute(array, "section", pairs)
        pairs = [
            (s * self.devices + i, ((s + by) % self.sections) * self.devices + j)
            for s in range(self.sections)
            for i, j in self.pairs(dy, 0, 0)
        ]
        return lax.ppermute(array, ("section", "expert"), pairs)

    def exchange(self, array):
        blocks = array.reshape(self.rows, -1, array.shape[-1])
        out = lax.all_to_all(
            blocks, "expert", 0, 0, tiled=True, axis_index_groups=self.row_groups
        )
        return out.reshape(array.shape)

    def near(self, mine):
        return self.move(mine, dx=1), self.move(mine, dx=-1)

    def far(self, left, right):
        middle = left.shape[0] // 2
        return self.move(left[:middle], dx=1), self.move(right[middle:], dx=-1)

    def swap(self, arrays):
        return [self.move(a, dc=1) for a in arrays]

    def collect(self, own, other):
        total = own.astype(f32) + other.astype(f32)
        rows = own.shape[0] // 4
        mine, left, right, far = [total[i * rows : (i + 1) * rows] for i in range(4)]
        middle = rows // 2
        far = far.astype(bf16)
        to_right = self.move(far[:middle], dx=1).astype(f32)
        to_left = self.move(far[middle:], dx=-1).astype(f32)
        right = jnp.concatenate([right[:middle] + to_right, right[middle:]], axis=0)
        left = jnp.concatenate([left[:middle], left[middle:] + to_left], axis=0)
        from_left = self.move(right.astype(bf16), dx=1).astype(f32)
        from_right = self.move(left.astype(bf16), dx=-1).astype(f32)
        return (mine + from_left + from_right).astype(bf16)


def block_of(array, index, rows, count=1):
    return lax.dynamic_slice_in_dim(array, index * rows, rows * count, axis=0)


def per_device(
    fwd_input,
    saved_input,
    out_cotangent,
    fwd_routes,
    bwd_routes,
    fwd_scores,
    bwd_scores,
    norm_gain,
    gate_proj,
    up_proj,
    down_proj,
):
    devices = lax.axis_size("expert")
    window = devices // GROUP
    net = Net(lax.axis_size("section"), devices, window)
    gate, up, down = gate_proj[0, 0], up_proj[0, 0], down_proj[0, 0]
    gain = norm_gain
    x_f, x_b, cot = fwd_input[0], saved_input[0], out_cotangent[0]
    routes_f, routes_b = fwd_routes[0].T, bwd_routes[0].T
    scores_f, scores_b = fwd_scores[0].T, bwd_scores[0].T
    width = x_f.shape[1]
    middle = x_f.shape[0] // 2
    row = lax.axis_index("expert") // GROUP
    cb, xs, cs, first, table, weights, inverse = prep_bwd(
        routes_b, scores_b, x_b, cot, gain, window
    )
    rows_f, mixing = prep_fwd(routes_f, scores_f, x_f, gain, window)

    mine_b = net.exchange(cb).reshape(window, 2, CAP, width)
    mine_b = mine_b.transpose(1, 0, 2, 3).reshape(cb.shape)
    top_f = net.relay(x_f[:middle], 1)
    top_c = net.relay(cot[:middle], -1)
    mixing = block_of(jnp.concatenate([mixing, mixing], axis=0), row, CAP, window)
    mixing = net.relay(mixing, 1)
    first = net.relay(first, -1)
    mine_b, rows_f, top_f, top_c, mixing, first = lax.optimization_barrier(
        (mine_b, rows_f, top_f, top_c, mixing, first)
    )

    left_b, right_b = net.near(mine_b)
    mine_f = net.exchange(rows_f)
    bottom_f = net.relay(after(x_f, rows_f)[middle:], 1)
    bottom_c = net.relay(after(cot, rows_f)[middle:], -1)
    left_b, right_b, mine_f, bottom_f, bottom_c = lax.optimization_barrier(
        (left_b, right_b, mine_f, bottom_f, bottom_c)
    )

    far_b = net.far(left_b, right_b)
    near_f = net.near(mine_f)
    near_b = [mine_b, left_b, right_b]
    near_b = near_b + net.swap(near_b)
    near_h = enter_bwd([(a, 0) for a in near_b], [(a, 1) for a in near_b], gate, up, down)
    far_b, near_f, near_h = lax.optimization_barrier((far_b, near_f, near_h))

    far_f = net.far(*near_f)
    own_f = [mine_f, *near_f, *far_f]
    far_b = [*far_b, *net.swap(far_b)]
    far_h = enter_bwd([(a, 0) for a in far_b[0::2]], [(a, 0) for a in far_b[1::2]], gate, up, down)
    own, peer = leave_bwd(near_h, far_h, gate, up)
    other = net.move(peer, dc=1)
    peer_f = net.swap(own_f)
    own, other, own_f, peer_f = lax.optimization_barrier((own, other, own_f, peer_f))

    dn = net.exchange(net.collect(own, other))
    own, peer = expert_fwd(own_f, peer_f, gate, up, down)
    outs = net.collect(own, net.move(peer, dc=1))
    outs = [
        net.relay(block_of(outs, lax.rem(row + window - d, window), CAP), 1, dy=-d)
        for d in range(window)
    ]
    grads, score_rows = grad_slots(
        routes_b, scores_b, table, weights, inverse, xs, cs, gain, dn
    )
    late_b = net.relay(grads, -1)
    fwd_handoff = place(place_fwd_kernel, "place_fwd", mixing, (top_f, bottom_f), *outs)
    grad_handoff = place(place_grad_kernel, "place_grad", first, (top_c, bottom_c), late_b)
    return (fwd_handoff[None], grad_handoff[None], score_rows.T[None])


def solution(mesh):
    tokens = P("section", "expert", None)
    slices = P("section", "expert", None, None)
    in_specs = (tokens,) * 7 + (P("section", None),) + (slices,) * 3
    return jax.shard_map(
        per_device, mesh=mesh, in_specs=in_specs, out_specs=(tokens,) * 3, check_vma=False
    )
```

```python
import functools

import jax
import jax.numpy as jnp
from jax import lax
from jax.experimental import pallas as pl
from jax.experimental.pallas import tpu as pltpu
from jax.sharding import PartitionSpec as P

GROUP = 8
CAP = 8
CORES = 2
LANES = 128
EPSILON = 1e-06
ROUTE_SCALE = 2.5
MIB = 1024 * 1024

bf16 = jnp.bfloat16
f32 = jnp.float32


def params(mib=24):
    return pltpu.CompilerParams(vmem_limit_bytes=mib * MIB)


def cost(flops, bytes_accessed):
    return pl.CostEstimate(flops=flops, bytes_accessed=bytes_accessed, transcendentals=0)


def dot(a, b, dims=((1,), (0,)), precision=None):
    return lax.dot_general(a, b, (dims, ((), ())), precision=precision, preferred_element_type=f32)


def exact(a, b, dims=((1,), (0,))):
    return dot(a, b, dims, lax.Precision.HIGHEST)


def sigmoid(v):
    return 1.0 / (1.0 + jnp.exp(-v))


def after(array, *others):
    return lax.optimization_barrier((array,) + others)[0]


def split_dot(weights, rows):
    high = weights.astype(bf16)
    low = (weights - high.astype(f32)).astype(bf16)
    return dot(high, rows) + dot(low, rows)


def slot_expert(slots, rows):
    return lax.broadcasted_iota(jnp.int32, (slots, rows), 0) // CAP


def gate_values(scores):
    affinity = sigmoid(scores)
    total = jnp.sum(affinity, axis=0, keepdims=True)
    return affinity, total, ROUTE_SCALE * affinity / total


def tables(routes, scores, slots):
    topk, rows = routes.shape
    expert = slot_expert(slots, rows)
    _, _, gates = gate_values(scores)
    naming = jnp.zeros((slots, rows), f32)
    weight = jnp.zeros((slots, rows), f32)
    for j in range(topk):
        hit = routes[j : j + 1, :] == expert
        naming = naming + jnp.where(hit, 1.0, 0.0)
        weight = weight + jnp.where(hit, gates[j : j + 1, :], 0.0)
    shape = (rows, rows)
    above = lax.broadcasted_iota(jnp.int32, shape, 0) < lax.broadcasted_iota(jnp.int32, shape, 1)
    earlier = dot(naming.astype(bf16), jnp.where(above, 1.0, 0.0).astype(bf16))
    slot = lax.rem(lax.broadcasted_iota(jnp.int32, (slots, rows), 0), CAP)
    here = earlier == slot.astype(f32)
    table = jnp.where(here, naming, 0.0)
    mixing = jnp.where(here, weight, 0.0)
    shape = (slots, slots)
    to = lax.broadcasted_iota(jnp.int32, shape, 0)
    from_ = lax.broadcasted_iota(jnp.int32, shape, 1)
    lower = (lax.rem(from_, CAP) == 0) & (from_ // CAP < to // CAP)
    before = dot(jnp.where(lower, 1.0, 0.0).astype(bf16), naming.astype(bf16))
    first = jnp.where(before == 0.0, table, 0.0)
    return table, mixing, first


def prep_bwd_kernel(
    steps, routes_ref, scores_ref, x_ref, cot_ref, gain_ref, cb_ref, xs_ref, cs_ref, first_ref,
    table_ref, weights_ref, inverse_ref, take_ref, x_slots_ref, c_slots_ref
):
    step = pl.program_id(0)
    slots = take_ref.shape[0]
    block = x_ref.shape[1]

    @pl.when(step == 0)
    def _():
        table, mixing, first = tables(routes_ref[...], scores_ref[...], slots)
        first_ref[...] = first
        table_ref[...] = table
        weights_ref[...] = exact(table, mixing, ((1,), (1,)))
        take_ref[...] = table.astype(bf16)

    take = take_ref[...]
    lanes = pl.ds(pl.multiple_of(step * block, LANES), block)
    x_slots_ref[:, lanes] = dot(take, x_ref[...])
    c_slots_ref[:, lanes] = dot(take, cot_ref[...])

    @pl.when(step == steps - 1)
    def _():
        x = x_slots_ref[...]
        c = c_slots_ref[...]
        inverse = lax.rsqrt(jnp.mean(x * x, axis=1, keepdims=True) + EPSILON)
        inverse_ref[...] = jnp.broadcast_to(inverse, inverse_ref.shape)
        normed = x * inverse * gain_ref[...]
        xs_ref[...] = x.astype(bf16)
        cs_ref[...] = c.astype(bf16)
        for k in range(slots // CAP):
            part = slice(k * CAP, (k + 1) * CAP)
            both = jnp.concatenate([c[part], normed[part]], axis=0).astype(bf16)
            cb_ref[2 * k * CAP : 2 * (k + 1) * CAP, :] = both


def prep_fwd_kernel(
    steps, routes_ref, scores_ref, x_ref, gain_ref, out_ref, mixing_ref, take_ref,
    x_slots_ref
):
    step = pl.program_id(0)
    slots = take_ref.shape[0]
    block = x_ref.shape[1]

    @pl.when(step == 0)
    def _():
        table, mixing, _ = tables(routes_ref[...], scores_ref[...], slots)
        mixing_ref[...] = mixing
        take_ref[...] = table.astype(bf16)

    lanes = pl.ds(pl.multiple_of(step * block, LANES), block)
    x_slots_ref[:, lanes] = dot(take_ref[...], x_ref[...])

    @pl.when(step == steps - 1)
    def _():
        x = x_slots_ref[...]
        inverse = lax.rsqrt(jnp.mean(x * x, axis=1, keepdims=True) + EPSILON)
        out_ref[...] = (x * inverse * gain_ref[...]).astype(bf16)


def vmem():
    return pl.BlockSpec(memory_space=pltpu.VMEM)


def whole(shape):
    return pl.BlockSpec(shape, lambda *_: (0,) * len(shape))


def across(rows, block):
    return pl.BlockSpec((rows, block), lambda i: (0, i))


def prep_bwd(routes, scores, x, cot, gain, window):
    rows, width = x.shape
    slots = window * CAP
    steps = 2
    block = width // steps
    shapes = [
        ((2 * slots, width), bf16),
        ((slots, width), bf16),
        ((slots, width), bf16),
        ((slots, rows), f32),
        ((slots, rows), f32),
        ((slots, slots), f32),
        ((slots, LANES), f32),
    ]
    return pl.pallas_call(
        functools.partial(prep_bwd_kernel, steps),
        out_shape=[jax.ShapeDtypeStruct(*s) for s in shapes],
        grid=(steps,),
        in_specs=[whole(routes.shape), whole(scores.shape)]
        + [across(rows, block)] * 2
        + [whole(gain.shape)],
        out_specs=[whole(s[0]) for s in shapes],
        scratch_shapes=[
            pltpu.VMEM((slots, rows), bf16),
            pltpu.VMEM((slots, width), f32),
            pltpu.VMEM((slots, width), f32),
        ],
        compiler_params=params(60),
        cost_estimate=cost(4 * slots * rows * width, 8 * rows * width),
        name="prep_bwd",
    )(routes, scores, x, cot, gain)


def prep_fwd(routes, scores, x, gain, window):
    rows, width = x.shape
    slots = window * CAP
    steps = 2
    block = width // steps
    return pl.pallas_call(
        functools.partial(prep_fwd_kernel, steps),
        out_shape=[
            jax.ShapeDtypeStruct((slots, width), bf16),
            jax.ShapeDtypeStruct((slots, rows), f32),
        ],
        grid=(steps,),
        in_specs=[whole(routes.shape), whole(scores.shape)]
        + [across(rows, block), whole(gain.shape)],
        out_specs=[whole((slots, width)), whole((slots, rows))],
        scratch_shapes=[pltpu.VMEM((slots, rows), bf16), pltpu.VMEM((slots, width), f32)],
        compiler_params=params(60),
        cost_estimate=cost(2 * slots * rows * width, 4 * rows * width),
        name="prep_fwd",
    )(routes, scores, x, gain)


def enter_bwd_kernel(steps, chunks, *refs):
    cot_refs, row_refs = refs[:chunks], refs[chunks : 2 * chunks]
    gate_ref, up_ref, down_ref, both_ref, dh_ref = refs[2 * chunks :]
    step = pl.program_id(0)
    weights = jnp.concatenate([gate_ref[...], up_ref[...]], axis=1)
    both = dot(jnp.concatenate([r[...] for r in row_refs], axis=0), weights)
    cots = jnp.concatenate([r[...] for r in cot_refs], axis=0)
    dh = dot(cots, down_ref[...], ((1,), (1,)))

    @pl.when(step == 0)
    def _():
        both_ref[...] = both
        dh_ref[...] = dh

    @pl.when(step > 0)
    def _():
        both_ref[...] += both
        dh_ref[...] += dh


def enter_bwd(cots, inputs, gate, up, down):
    width, hidden = gate.shape
    steps = 2
    block = width // steps
    part = 32
    total = len(cots) * part
    pick = lambda k: pl.BlockSpec((part, block), lambda i: (k, i))
    return pl.pallas_call(
        functools.partial(enter_bwd_kernel, steps, len(cots)),
        out_shape=[
            jax.ShapeDtypeStruct((total, 2 * hidden), f32),
            jax.ShapeDtypeStruct((total, hidden), f32),
        ],
        grid=(steps,),
        in_specs=[pick(k) for _, k in cots + inputs]
        + [pl.BlockSpec((block, hidden), lambda i: (i, 0))] * 2
        + [pl.BlockSpec((hidden, block), lambda i: (0, i))],
        out_specs=[whole((total, 2 * hidden)), whole((total, hidden))],
        compiler_params=params(),
        cost_estimate=cost(6 * total * width * hidden, 4 * total * width + 6 * width * hidden),
        name="enter_bwd",
    )(*[a for a, _ in cots + inputs], gate, up, down)


def leave_bwd_kernel(steps, near_both, near_dh, far_both, far_dh, gate_ref, up_ref, *refs):
    own_ref, peer_ref, da_ref, q_ref = refs
    step = pl.program_id(0)
    hidden = gate_ref.shape[1]
    block = gate_ref.shape[0]

    @pl.when(step == 0)
    def _():
        n, m = near_dh.shape[0] // 2, far_dh.shape[0] // 2

        def joined(a, b):
            return jnp.concatenate([a[:n], b[:m], a[n:], b[m:]], axis=0)

        both = joined(near_both[...], far_both[...])
        dh = joined(near_dh[...], far_dh[...])
        pre_gate = both[:, :hidden]
        pre_up = both[:, hidden:]
        sig = sigmoid(pre_gate)
        active = pre_gate * sig
        h = (active * pre_up).astype(bf16).astype(f32)
        da = dh * pre_up * sig * (1.0 + pre_gate * (1.0 - sig))
        db = dh * active
        da_ref[...] = jnp.concatenate([da, db], axis=1).astype(bf16)
        q = jnp.sum(dh * h, axis=1, keepdims=True)
        q_ref[...] = jnp.broadcast_to(q, q_ref.shape).astype(bf16)

    weights = jnp.concatenate([gate_ref[...], up_ref[...]], axis=1)
    grads = dot(da_ref[...], weights, ((1,), (1,))).astype(bf16)
    lanes = pl.ds(pl.multiple_of(step * block, LANES), block)
    middle = grads.shape[0] // 2
    own_ref[:, lanes] = grads[:middle]
    peer_ref[:, lanes] = grads[middle:]

    @pl.when(step == steps - 1)
    def _():
        own_ref[:, steps * block :] = q_ref[:middle, :]
        peer_ref[:, steps * block :] = q_ref[middle:, :]


def leave_bwd(near, far, gate, up):
    width, hidden = gate.shape
    steps = 2
    block = width // steps
    total = near[1].shape[0] + far[1].shape[0]
    out = jax.ShapeDtypeStruct((total // 2, width + LANES), bf16)
    small = [*near, *far]
    return pl.pallas_call(
        functools.partial(leave_bwd_kernel, steps),
        out_shape=[out, out],
        grid=(steps,),
        in_specs=[whole(a.shape) for a in small]
        + [pl.BlockSpec((block, hidden), lambda i: (i, 0))] * 2,
        out_specs=[whole(out.shape)] * 2,
        scratch_shapes=[pltpu.VMEM((total, 2 * hidden), bf16), pltpu.VMEM((total, LANES), bf16)],
        compiler_params=params(),
        cost_estimate=cost(4 * total * width * hidden, 2 * total * width + 4 * width * hidden),
        name="leave_bwd",
    )(*small, gate, up)


def expert_fwd_kernel(steps, chunks, *refs):
    rows_refs = refs[:chunks]
    gate_ref, up_ref, down_ref, own_ref, peer_ref, both_ref, h_ref = refs[chunks:]
    step = pl.program_id(0)
    hidden = gate_ref.shape[1]
    block = gate_ref.shape[0]

    @pl.when(step < steps)
    def _():
        weights = jnp.concatenate([gate_ref[...], up_ref[...]], axis=1)
        both = dot(jnp.concatenate([r[...] for r in rows_refs], axis=0), weights)

        @pl.when(step == 0)
        def _():
            both_ref[...] = both

        @pl.when(step > 0)
        def _():
            both_ref[...] += both

    @pl.when(step == steps - 1)
    def _():
        pre_gate = both_ref[:, :hidden]
        h_ref[...] = (pre_gate * sigmoid(pre_gate) * both_ref[:, hidden:]).astype(bf16)

    @pl.when(step >= steps)
    def _():
        outs = dot(h_ref[...], down_ref[...]).astype(bf16)
        lanes = pl.ds(pl.multiple_of((step - steps) * block, LANES), block)
        middle = outs.shape[0] // 2
        own_ref[:, lanes] = outs[:middle]
        peer_ref[:, lanes] = outs[middle:]


def expert_fwd(own, peer, gate, up, down):
    width, hidden = gate.shape
    steps = 2
    block = width // steps
    chunks = own + peer
    rows = sum(c.shape[0] for c in own)
    take = lambda i: jnp.minimum(i, steps - 1)
    out = jax.ShapeDtypeStruct((rows, width), bf16)
    return pl.pallas_call(
        functools.partial(expert_fwd_kernel, steps, len(chunks)),
        out_shape=[out, out],
        grid=(2 * steps,),
        in_specs=[pl.BlockSpec((c.shape[0], block), lambda i: (0, take(i))) for c in chunks]
        + [
            pl.BlockSpec((block, hidden), lambda i: (take(i), 0)),
            pl.BlockSpec((block, hidden), lambda i: (take(i), 0)),
            pl.BlockSpec((hidden, block), lambda i: (0, jnp.maximum(i - steps, 0))),
        ],
        out_specs=[whole(out.shape)] * 2,
        scratch_shapes=[
            pltpu.VMEM((2 * rows, 2 * hidden), f32),
            pltpu.VMEM((2 * rows, hidden), bf16),
        ],
        compiler_params=params(),
        cost_estimate=cost(12 * rows * width * hidden, 8 * rows * width + 6 * width * hidden),
        name="expert_fwd",
    )(*chunks, gate, up, down)


def grad_slots_kernel(
    routes_ref, scores_ref, table_ref, weights_ref, inverse_ref, xs_ref, cs_ref, gain_ref, dn_ref,
    grad_ref, score_ref
):
    slots, width = xs_ref.shape
    t = split_dot(weights_ref[...], dn_ref[:, :width]) * gain_ref[...]
    x = xs_ref[...].astype(f32)
    inverse = inverse_ref[:, :1]
    mean = jnp.mean(x * t, axis=1, keepdims=True)
    grad = cs_ref[...].astype(f32) + inverse * t - x * (inverse * inverse * inverse * mean)
    grad_ref[...] = grad.astype(bf16)

    routes = routes_ref[...]
    topk, rows = routes.shape
    spread = table_ref[...] * dn_ref[:, width:].astype(f32)[:, :1]
    expert = slot_expert(slots, rows)
    place = lax.broadcasted_iota(jnp.int32, (topk, rows), 0)
    dgate = jnp.zeros((topk, rows), f32)
    for j in range(topk):
        hit = routes[j : j + 1, :] == expert
        value = jnp.sum(jnp.where(hit, spread, 0.0), axis=0, keepdims=True)
        dgate = jnp.where(place == j, value, dgate)
    affinity, total, gates = gate_values(scores_ref[...])
    term = jnp.sum(dgate * gates, axis=0, keepdims=True) / ROUTE_SCALE
    score_ref[...] = affinity * (1.0 - affinity) * (ROUTE_SCALE / total) * (dgate - term)


def grad_slots(routes, scores, table, weights, inverse, xs, cs, gain, dn):
    slots, width = xs.shape
    return pl.pallas_call(
        grad_slots_kernel,
        out_shape=[
            jax.ShapeDtypeStruct((slots, width), bf16),
            jax.ShapeDtypeStruct(scores.shape, f32),
        ],
        in_specs=[vmem()] * 9,
        out_specs=[vmem()] * 2,
        compiler_params=params(),
        cost_estimate=cost(4 * slots * slots * width, 8 * slots * width),
        name="grad_slots",
    )(routes, scores, table, weights, inverse, xs, cs, gain, dn)


def stacked(refs):
    return jnp.concatenate([r[...].astype(f32) for r in refs], axis=0)


def place_grad_kernel(first_ref, top_ref, bottom_ref, slots_ref, out_ref):
    first = first_ref[...].astype(bf16)
    touched = dot(first, jnp.ones((first.shape[0], LANES), bf16), ((0,), (0,)))[:, :1]
    placed = dot(first, slots_ref[...], ((0,), (0,)))
    out_ref[...] = jnp.where(touched > 0.0, placed, stacked([top_ref, bottom_ref])).astype(bf16)


def place_fwd_kernel(mixing_ref, early_ref, *refs):
    out_ref = refs[-1]
    mixing = mixing_ref[...]
    high = mixing.astype(bf16)
    low = (mixing - high.astype(f32)).astype(bf16)
    rows = stacked(refs[:-1]).astype(bf16)
    branch = dot(high, rows, ((0,), (0,))) + dot(low, rows, ((0,), (0,)))
    out_ref[...] = (early_ref[...].astype(f32) + branch).astype(bf16)


def place(kernel, name, table, early, *blocks):
    slots, rows = table.shape
    width = early[0].shape[1]
    steps = 2
    block = width // steps
    return pl.pallas_call(
        kernel,
        out_shape=jax.ShapeDtypeStruct((rows, width), bf16),
        grid=(steps,),
        in_specs=[whole(table.shape)] + [across(b.shape[0], block) for b in [*early, *blocks]],
        out_specs=across(rows, block),
        compiler_params=params(),
        cost_estimate=cost(4 * rows * slots * width, 6 * rows * width),
        name=name,
    )(table, *early, *blocks)


class Net:
    def __init__(self, sections, devices, window):
        self.sections, self.devices = sections, devices
        self.rows = window
        self.columns = devices // window // CORES
        self.row_groups = [
            [self.index(y, x, c) for y in range(self.rows)]
            for x in range(self.columns)
            for c in range(CORES)
        ]

    def index(self, y, x, c):
        return ((y % self.rows) * self.columns + x % self.columns) * CORES + c % CORES

    def pairs(self, dy, dx, dc):
        return [
            (self.index(y, x, c), self.index(y + dy, x + dx, c + dc))
            for y in range(self.rows)
            for x in range(self.columns)
            for c in range(CORES)
        ]

    def move(self, array, dy=0, dx=0, dc=0):
        return lax.ppermute(array, "expert", self.pairs(dy, dx, dc))

    def relay(self, array, by, dy=0):
        if dy == 0:
            pairs = [(s, (s + by) % self.sections) for s in range(self.sections)]
            return lax.ppermute(array, "section", pairs)
        pairs = [
            (s * self.devices + i, ((s + by) % self.sections) * self.devices + j)
            for s in range(self.sections)
            for i, j in self.pairs(dy, 0, 0)
        ]
        return lax.ppermute(array, ("section", "expert"), pairs)

    def exchange(self, array):
        blocks = array.reshape(self.rows, -1, array.shape[-1])
        out = lax.all_to_all(
            blocks, "expert", 0, 0, tiled=True, axis_index_groups=self.row_groups
        )
        return out.reshape(array.shape)

    def near(self, mine):
        return self.move(mine, dx=1), self.move(mine, dx=-1)

    def far(self, left, right):
        middle = left.shape[0] // 2
        return self.move(left[:middle], dx=1), self.move(right[middle:], dx=-1)

    def swap(self, arrays):
        return [self.move(a, dc=1) for a in arrays]

    def collect(self, own, other):
        total = own.astype(f32) + other.astype(f32)
        rows = own.shape[0] // 4
        mine, left, right, far = [total[i * rows : (i + 1) * rows] for i in range(4)]
        middle = rows // 2
        far = far.astype(bf16)
        to_right = self.move(far[:middle], dx=1).astype(f32)
        to_left = self.move(far[middle:], dx=-1).astype(f32)
        right = jnp.concatenate([right[:middle] + to_right, right[middle:]], axis=0)
        left = jnp.concatenate([left[:middle], left[middle:] + to_left], axis=0)
        from_left = self.move(right.astype(bf16), dx=1).astype(f32)
        from_right = self.move(left.astype(bf16), dx=-1).astype(f32)
        return (mine + from_left + from_right).astype(bf16)


def block_of(array, index, rows, count=1):
    return lax.dynamic_slice_in_dim(array, index * rows, rows * count, axis=0)


def per_device(
    fwd_input,
    saved_input,
    out_cotangent,
    fwd_routes,
    bwd_routes,
    fwd_scores,
    bwd_scores,
    norm_gain,
    gate_proj,
    up_proj,
    down_proj,
):
    devices = lax.axis_size("expert")
    window = devices // GROUP
    net = Net(lax.axis_size("section"), devices, window)
    gate, up, down = gate_proj[0, 0], up_proj[0, 0], down_proj[0, 0]
    gain = norm_gain
    x_f, x_b, cot = fwd_input[0], saved_input[0], out_cotangent[0]
    routes_f, routes_b = fwd_routes[0].T, bwd_routes[0].T
    scores_f, scores_b = fwd_scores[0].T, bwd_scores[0].T
    width = x_f.shape[1]
    middle = x_f.shape[0] // 2
    row = lax.axis_index("expert") // GROUP
    cb, xs, cs, first, table, weights, inverse = prep_bwd(
        routes_b, scores_b, x_b, cot, gain, window
    )
    rows_f, mixing = prep_fwd(routes_f, scores_f, x_f, gain, window)

    mine_b = net.exchange(cb).reshape(window, 2, CAP, width)
    mine_b = mine_b.transpose(1, 0, 2, 3).reshape(cb.shape)
    mine_b, rows_f = lax.optimization_barrier((mine_b, rows_f))

    left_b, right_b = net.near(mine_b)
    mine_f = net.exchange(rows_f)
    early_f = net.relay(x_f, 1)
    top_c = net.relay(cot[:middle], -1)
    mixing = block_of(jnp.concatenate([mixing, mixing], axis=0), row, CAP, window)
    mixing = net.relay(mixing, 1)
    first = net.relay(first, -1)
    left_b, right_b, mine_f, early_f, top_c, mixing, first = lax.optimization_barrier(
        (left_b, right_b, mine_f, early_f, top_c, mixing, first)
    )

    far_b = net.far(left_b, right_b)
    near_f = net.near(mine_f)
    near_b = [mine_b, left_b, right_b]
    near_b = near_b + net.swap(near_b)
    bottom_c = net.relay(after(cot, near_b[5])[middle:], -1)
    near_h = enter_bwd([(a, 0) for a in near_b], [(a, 1) for a in near_b], gate, up, down)
    far_b, near_f, near_h, bottom_c = lax.optimization_barrier((far_b, near_f, near_h, bottom_c))

    far_f = net.far(*near_f)
    far_b = [*far_b, *net.swap(far_b)]
    far_h = enter_bwd([(a, 0) for a in far_b[0::2]], [(a, 0) for a in far_b[1::2]], gate, up, down)
    own, peer = leave_bwd(near_h, far_h, gate, up)
    other = net.move(peer, dc=1)
    own, other, far_f = lax.optimization_barrier((own, other, far_f))

    dn = net.exchange(net.collect(own, other))
    own_f = [mine_f, *near_f, *far_f]
    own, peer = expert_fwd(own_f, net.swap(own_f), gate, up, down)
    outs = net.collect(own, net.move(peer, dc=1))
    outs = [
        net.relay(block_of(outs, lax.rem(row + window - d, window), CAP), 1, dy=-d)
        for d in range(window)
    ]
    grads, score_rows = grad_slots(
        routes_b, scores_b, table, weights, inverse, xs, cs, gain, dn
    )
    late_b = net.relay(grads, -1)
    fwd_handoff = place(place_fwd_kernel, "place_fwd", mixing, (early_f,), *outs)
    grad_handoff = place(place_grad_kernel, "place_grad", first, (top_c, bottom_c), late_b)
    return (fwd_handoff[None], grad_handoff[None], score_rows.T[None])


def solution(mesh):
    tokens = P("section", "expert", None)
    slices = P("section", "expert", None, None)
    in_specs = (tokens,) * 7 + (P("section", None),) + (slices,) * 3
    return jax.shard_map(
        per_device, mesh=mesh, in_specs=in_specs, out_specs=(tokens,) * 3, check_vma=False
    )
```

```python
import functools

import jax
import jax.numpy as jnp
from jax import lax
from jax.experimental import pallas as pl
from jax.experimental.pallas import tpu as pltpu
from jax.sharding import PartitionSpec as P

GROUP = 8
CAP = 8
CORES = 2
LANES = 128
EPSILON = 1e-06
ROUTE_SCALE = 2.5
MIB = 1024 * 1024

bf16 = jnp.bfloat16
f32 = jnp.float32


def params(mib=24):
    return pltpu.CompilerParams(vmem_limit_bytes=mib * MIB)


def cost(flops, bytes_accessed):
    return pl.CostEstimate(flops=flops, bytes_accessed=bytes_accessed, transcendentals=0)


def dot(a, b, dims=((1,), (0,)), precision=None):
    return lax.dot_general(a, b, (dims, ((), ())), precision=precision, preferred_element_type=f32)


def exact(a, b, dims=((1,), (0,))):
    return dot(a, b, dims, lax.Precision.HIGHEST)


def sigmoid(v):
    return 1.0 / (1.0 + jnp.exp(-v))


def after(array, *others):
    return lax.optimization_barrier((array,) + others)[0]


def split_dot(weights, rows):
    high = weights.astype(bf16)
    low = (weights - high.astype(f32)).astype(bf16)
    return dot(high, rows) + dot(low, rows)


def slot_expert(slots, rows):
    return lax.broadcasted_iota(jnp.int32, (slots, rows), 0) // CAP


def gate_values(scores):
    affinity = sigmoid(scores)
    total = jnp.sum(affinity, axis=0, keepdims=True)
    return affinity, total, ROUTE_SCALE * affinity / total


def tables(routes, scores, slots):
    topk, rows = routes.shape
    expert = slot_expert(slots, rows)
    _, _, gates = gate_values(scores)
    naming = jnp.zeros((slots, rows), f32)
    weight = jnp.zeros((slots, rows), f32)
    for j in range(topk):
        hit = routes[j : j + 1, :] == expert
        naming = naming + jnp.where(hit, 1.0, 0.0)
        weight = weight + jnp.where(hit, gates[j : j + 1, :], 0.0)
    shape = (rows, rows)
    above = lax.broadcasted_iota(jnp.int32, shape, 0) < lax.broadcasted_iota(jnp.int32, shape, 1)
    earlier = dot(naming.astype(bf16), jnp.where(above, 1.0, 0.0).astype(bf16))
    slot = lax.rem(lax.broadcasted_iota(jnp.int32, (slots, rows), 0), CAP)
    here = earlier == slot.astype(f32)
    table = jnp.where(here, naming, 0.0)
    mixing = jnp.where(here, weight, 0.0)
    shape = (slots, slots)
    to = lax.broadcasted_iota(jnp.int32, shape, 0)
    from_ = lax.broadcasted_iota(jnp.int32, shape, 1)
    lower = (lax.rem(from_, CAP) == 0) & (from_ // CAP < to // CAP)
    before = dot(jnp.where(lower, 1.0, 0.0).astype(bf16), naming.astype(bf16))
    first = jnp.where(before == 0.0, table, 0.0)
    return table, mixing, first


def prep_bwd_kernel(
    steps, routes_ref, scores_ref, x_ref, cot_ref, gain_ref, cb_ref, xs_ref, cs_ref, first_ref,
    table_ref, weights_ref, inverse_ref, take_ref, x_slots_ref, c_slots_ref
):
    step = pl.program_id(0)
    slots = take_ref.shape[0]
    block = x_ref.shape[1]

    @pl.when(step == 0)
    def _():
        table, mixing, first = tables(routes_ref[...], scores_ref[...], slots)
        first_ref[...] = jnp.zeros(first_ref.shape, f32)
        first_ref[:, : table.shape[1]] = first
        table_ref[...] = table
        weights_ref[...] = exact(table, mixing, ((1,), (1,)))
        take_ref[...] = table.astype(bf16)

    take = take_ref[...]
    lanes = pl.ds(pl.multiple_of(step * block, LANES), block)
    x_slots_ref[:, lanes] = dot(take, x_ref[...])
    c_slots_ref[:, lanes] = dot(take, cot_ref[...])

    @pl.when(step == steps - 1)
    def _():
        x = x_slots_ref[...]
        c = c_slots_ref[...]
        inverse = lax.rsqrt(jnp.mean(x * x, axis=1, keepdims=True) + EPSILON)
        inverse_ref[...] = jnp.broadcast_to(inverse, inverse_ref.shape)
        normed = x * inverse * gain_ref[...]
        xs_ref[...] = x.astype(bf16)
        cs_ref[...] = c.astype(bf16)
        for k in range(slots // CAP):
            part = slice(k * CAP, (k + 1) * CAP)
            both = jnp.concatenate([c[part], normed[part]], axis=0).astype(bf16)
            cb_ref[2 * k * CAP : 2 * (k + 1) * CAP, :] = both


def prep_fwd_kernel(
    steps, routes_ref, scores_ref, x_ref, gain_ref, out_ref, mixing_ref, take_ref,
    x_slots_ref
):
    step = pl.program_id(0)
    slots = take_ref.shape[0]
    block = x_ref.shape[1]

    @pl.when(step == 0)
    def _():
        table, mixing, _ = tables(routes_ref[...], scores_ref[...], slots)
        mixing_ref[...] = mixing
        take_ref[...] = table.astype(bf16)

    lanes = pl.ds(pl.multiple_of(step * block, LANES), block)
    x_slots_ref[:, lanes] = dot(take_ref[...], x_ref[...])

    @pl.when(step == steps - 1)
    def _():
        x = x_slots_ref[...]
        inverse = lax.rsqrt(jnp.mean(x * x, axis=1, keepdims=True) + EPSILON)
        out_ref[...] = (x * inverse * gain_ref[...]).astype(bf16)


def vmem():
    return pl.BlockSpec(memory_space=pltpu.VMEM)


def whole(shape):
    return pl.BlockSpec(shape, lambda *_: (0,) * len(shape))


def across(rows, block):
    return pl.BlockSpec((rows, block), lambda i: (0, i))


def prep_bwd(routes, scores, x, cot, gain, window):
    rows, width = x.shape
    slots = window * CAP
    steps = 2
    block = width // steps
    shapes = [
        ((2 * slots, width), bf16),
        ((slots, width), bf16),
        ((slots, width), bf16),
        ((slots, LANES), f32),
        ((slots, rows), f32),
        ((slots, slots), f32),
        ((slots, LANES), f32),
    ]
    return pl.pallas_call(
        functools.partial(prep_bwd_kernel, steps),
        out_shape=[jax.ShapeDtypeStruct(*s) for s in shapes],
        grid=(steps,),
        in_specs=[whole(routes.shape), whole(scores.shape)]
        + [across(rows, block)] * 2
        + [whole(gain.shape)],
        out_specs=[whole(s[0]) for s in shapes],
        scratch_shapes=[
            pltpu.VMEM((slots, rows), bf16),
            pltpu.VMEM((slots, width), f32),
            pltpu.VMEM((slots, width), f32),
        ],
        compiler_params=params(60),
        cost_estimate=cost(4 * slots * rows * width, 8 * rows * width),
        name="prep_bwd",
    )(routes, scores, x, cot, gain)


def prep_fwd(routes, scores, x, gain, window):
    rows, width = x.shape
    slots = window * CAP
    steps = 2
    block = width // steps
    return pl.pallas_call(
        functools.partial(prep_fwd_kernel, steps),
        out_shape=[
            jax.ShapeDtypeStruct((slots, width), bf16),
            jax.ShapeDtypeStruct((slots, rows), f32),
        ],
        grid=(steps,),
        in_specs=[whole(routes.shape), whole(scores.shape)]
        + [across(rows, block), whole(gain.shape)],
        out_specs=[whole((slots, width)), whole((slots, rows))],
        scratch_shapes=[pltpu.VMEM((slots, rows), bf16), pltpu.VMEM((slots, width), f32)],
        compiler_params=params(60),
        cost_estimate=cost(2 * slots * rows * width, 4 * rows * width),
        name="prep_fwd",
    )(routes, scores, x, gain)


def enter_bwd_kernel(steps, chunks, *refs):
    cot_refs, row_refs = refs[:chunks], refs[chunks : 2 * chunks]
    gate_ref, up_ref, down_ref, both_ref, dh_ref = refs[2 * chunks :]
    step = pl.program_id(0)
    weights = jnp.concatenate([gate_ref[...], up_ref[...]], axis=1)
    both = dot(jnp.concatenate([r[...] for r in row_refs], axis=0), weights)
    cots = jnp.concatenate([r[...] for r in cot_refs], axis=0)
    dh = dot(cots, down_ref[...], ((1,), (1,)))

    @pl.when(step == 0)
    def _():
        both_ref[...] = both
        dh_ref[...] = dh

    @pl.when(step > 0)
    def _():
        both_ref[...] += both
        dh_ref[...] += dh


def enter_bwd(cots, inputs, gate, up, down):
    width, hidden = gate.shape
    steps = 2
    block = width // steps
    part = 32
    total = len(cots) * part
    pick = lambda k: pl.BlockSpec((part, block), lambda i: (k, i))
    return pl.pallas_call(
        functools.partial(enter_bwd_kernel, steps, len(cots)),
        out_shape=[
            jax.ShapeDtypeStruct((total, 2 * hidden), f32),
            jax.ShapeDtypeStruct((total, hidden), f32),
        ],
        grid=(steps,),
        in_specs=[pick(k) for _, k in cots + inputs]
        + [pl.BlockSpec((block, hidden), lambda i: (i, 0))] * 2
        + [pl.BlockSpec((hidden, block), lambda i: (0, i))],
        out_specs=[whole((total, 2 * hidden)), whole((total, hidden))],
        compiler_params=params(),
        cost_estimate=cost(6 * total * width * hidden, 4 * total * width + 6 * width * hidden),
        name="enter_bwd",
    )(*[a for a, _ in cots + inputs], gate, up, down)


def leave_bwd_kernel(steps, near_both, near_dh, far_both, far_dh, gate_ref, up_ref, *refs):
    own_ref, peer_ref, da_ref, q_ref = refs
    step = pl.program_id(0)
    hidden = gate_ref.shape[1]
    block = gate_ref.shape[0]

    @pl.when(step == 0)
    def _():
        n, m = near_dh.shape[0] // 2, far_dh.shape[0] // 2

        def joined(a, b):
            return jnp.concatenate([a[:n], b[:m], a[n:], b[m:]], axis=0)

        both = joined(near_both[...], far_both[...])
        dh = joined(near_dh[...], far_dh[...])
        pre_gate = both[:, :hidden]
        pre_up = both[:, hidden:]
        sig = sigmoid(pre_gate)
        active = pre_gate * sig
        h = (active * pre_up).astype(bf16).astype(f32)
        da = dh * pre_up * sig * (1.0 + pre_gate * (1.0 - sig))
        db = dh * active
        da_ref[...] = jnp.concatenate([da, db], axis=1).astype(bf16)
        q = jnp.sum(dh * h, axis=1, keepdims=True)
        q_ref[...] = jnp.broadcast_to(q, q_ref.shape).astype(bf16)

    weights = jnp.concatenate([gate_ref[...], up_ref[...]], axis=1)
    grads = dot(da_ref[...], weights, ((1,), (1,))).astype(bf16)
    lanes = pl.ds(pl.multiple_of(step * block, LANES), block)
    middle = grads.shape[0] // 2
    own_ref[:, lanes] = grads[:middle]
    peer_ref[:, lanes] = grads[middle:]

    @pl.when(step == steps - 1)
    def _():
        own_ref[:, steps * block :] = q_ref[:middle, :]
        peer_ref[:, steps * block :] = q_ref[middle:, :]


def leave_bwd(near, far, gate, up):
    width, hidden = gate.shape
    steps = 2
    block = width // steps
    total = near[1].shape[0] + far[1].shape[0]
    out = jax.ShapeDtypeStruct((total // 2, width + LANES), bf16)
    small = [*near, *far]
    return pl.pallas_call(
        functools.partial(leave_bwd_kernel, steps),
        out_shape=[out, out],
        grid=(steps,),
        in_specs=[whole(a.shape) for a in small]
        + [pl.BlockSpec((block, hidden), lambda i: (i, 0))] * 2,
        out_specs=[whole(out.shape)] * 2,
        scratch_shapes=[pltpu.VMEM((total, 2 * hidden), bf16), pltpu.VMEM((total, LANES), bf16)],
        compiler_params=params(),
        cost_estimate=cost(4 * total * width * hidden, 2 * total * width + 4 * width * hidden),
        name="leave_bwd",
    )(*small, gate, up)


def expert_fwd_kernel(steps, chunks, *refs):
    rows_refs = refs[:chunks]
    gate_ref, up_ref, down_ref, own_ref, peer_ref, both_ref, h_ref = refs[chunks:]
    step = pl.program_id(0)
    hidden = gate_ref.shape[1]
    block = gate_ref.shape[0]

    @pl.when(step < steps)
    def _():
        weights = jnp.concatenate([gate_ref[...], up_ref[...]], axis=1)
        both = dot(jnp.concatenate([r[...] for r in rows_refs], axis=0), weights)

        @pl.when(step == 0)
        def _():
            both_ref[...] = both

        @pl.when(step > 0)
        def _():
            both_ref[...] += both

    @pl.when(step == steps - 1)
    def _():
        pre_gate = both_ref[:, :hidden]
        h_ref[...] = (pre_gate * sigmoid(pre_gate) * both_ref[:, hidden:]).astype(bf16)

    @pl.when(step >= steps)
    def _():
        outs = dot(h_ref[...], down_ref[...]).astype(bf16)
        lanes = pl.ds(pl.multiple_of((step - steps) * block, LANES), block)
        middle = outs.shape[0] // 2
        own_ref[:, lanes] = outs[:middle]
        peer_ref[:, lanes] = outs[middle:]


def expert_fwd(own, peer, gate, up, down):
    width, hidden = gate.shape
    steps = 2
    block = width // steps
    chunks = own + peer
    rows = sum(c.shape[0] for c in own)
    take = lambda i: jnp.minimum(i, steps - 1)
    out = jax.ShapeDtypeStruct((rows, width), bf16)
    return pl.pallas_call(
        functools.partial(expert_fwd_kernel, steps, len(chunks)),
        out_shape=[out, out],
        grid=(2 * steps,),
        in_specs=[pl.BlockSpec((c.shape[0], block), lambda i: (0, take(i))) for c in chunks]
        + [
            pl.BlockSpec((block, hidden), lambda i: (take(i), 0)),
            pl.BlockSpec((block, hidden), lambda i: (take(i), 0)),
            pl.BlockSpec((hidden, block), lambda i: (0, jnp.maximum(i - steps, 0))),
        ],
        out_specs=[whole(out.shape)] * 2,
        scratch_shapes=[
            pltpu.VMEM((2 * rows, 2 * hidden), f32),
            pltpu.VMEM((2 * rows, hidden), bf16),
        ],
        compiler_params=params(),
        cost_estimate=cost(12 * rows * width * hidden, 8 * rows * width + 6 * width * hidden),
        name="expert_fwd",
    )(*chunks, gate, up, down)


def grad_slots_kernel(
    routes_ref, scores_ref, table_ref, first_ref, weights_ref, inverse_ref, xs_ref, cs_ref, gain_ref, dn_ref,
    grad_ref, score_ref
):
    slots, width = xs_ref.shape
    t = split_dot(weights_ref[...], dn_ref[:, :width]) * gain_ref[...]
    x = xs_ref[...].astype(f32)
    inverse = inverse_ref[:, :1]
    mean = jnp.mean(x * t, axis=1, keepdims=True)
    grad = cs_ref[...].astype(f32) + inverse * t - x * (inverse * inverse * inverse * mean)
    grad_ref[:, :width] = grad.astype(bf16)
    grad_ref[:, width:] = first_ref[...].astype(bf16)

    routes = routes_ref[...]
    topk, rows = routes.shape
    spread = table_ref[...] * dn_ref[:, width:].astype(f32)[:, :1]
    expert = slot_expert(slots, rows)
    place = lax.broadcasted_iota(jnp.int32, (topk, rows), 0)
    dgate = jnp.zeros((topk, rows), f32)
    for j in range(topk):
        hit = routes[j : j + 1, :] == expert
        value = jnp.sum(jnp.where(hit, spread, 0.0), axis=0, keepdims=True)
        dgate = jnp.where(place == j, value, dgate)
    affinity, total, gates = gate_values(scores_ref[...])
    term = jnp.sum(dgate * gates, axis=0, keepdims=True) / ROUTE_SCALE
    score_ref[...] = affinity * (1.0 - affinity) * (ROUTE_SCALE / total) * (dgate - term)


def grad_slots(routes, scores, table, first, weights, inverse, xs, cs, gain, dn):
    slots, width = xs.shape
    return pl.pallas_call(
        grad_slots_kernel,
        out_shape=[
            jax.ShapeDtypeStruct((slots, width + LANES), bf16),
            jax.ShapeDtypeStruct(scores.shape, f32),
        ],
        in_specs=[vmem()] * 10,
        out_specs=[vmem()] * 2,
        compiler_params=params(),
        cost_estimate=cost(4 * slots * slots * width, 8 * slots * width),
        name="grad_slots",
    )(routes, scores, table, first, weights, inverse, xs, cs, gain, dn)


def stacked(refs):
    return jnp.concatenate([r[...].astype(f32) for r in refs], axis=0)


def place_grad_kernel(top_ref, bottom_ref, slots_ref, first_ref, out_ref):
    rows = out_ref.shape[0]
    first = first_ref[...][:, :rows]
    touched = dot(first, jnp.ones((first.shape[0], LANES), bf16), ((0,), (0,)))[:, :1]
    placed = dot(first, slots_ref[...], ((0,), (0,)))
    out_ref[...] = jnp.where(touched > 0.0, placed, stacked([top_ref, bottom_ref])).astype(bf16)


def place_grad(early, late):
    width = early[0].shape[1]
    rows = sum(e.shape[0] for e in early)
    slots = late.shape[0]
    steps = 2
    block = width // steps
    return pl.pallas_call(
        place_grad_kernel,
        out_shape=jax.ShapeDtypeStruct((rows, width), bf16),
        grid=(steps,),
        in_specs=[across(e.shape[0], block) for e in early]
        + [across(slots, block), pl.BlockSpec((slots, LANES), lambda i: (0, width // LANES))],
        out_specs=across(rows, block),
        compiler_params=params(),
        cost_estimate=cost(2 * rows * slots * width, 6 * rows * width),
        name="place_grad",
    )(*early, late, late)


def place_fwd_kernel(mixing_ref, early_ref, *refs):
    out_ref = refs[-1]
    mixing = mixing_ref[...]
    high = mixing.astype(bf16)
    low = (mixing - high.astype(f32)).astype(bf16)
    rows = stacked(refs[:-1]).astype(bf16)
    branch = dot(high, rows, ((0,), (0,))) + dot(low, rows, ((0,), (0,)))
    out_ref[...] = (early_ref[...].astype(f32) + branch).astype(bf16)


def place(kernel, name, table, early, *blocks):
    slots, rows = table.shape
    width = early[0].shape[1]
    steps = 2
    block = width // steps
    return pl.pallas_call(
        kernel,
        out_shape=jax.ShapeDtypeStruct((rows, width), bf16),
        grid=(steps,),
        in_specs=[whole(table.shape)] + [across(b.shape[0], block) for b in [*early, *blocks]],
        out_specs=across(rows, block),
        compiler_params=params(),
        cost_estimate=cost(4 * rows * slots * width, 6 * rows * width),
        name=name,
    )(table, *early, *blocks)


class Net:
    def __init__(self, sections, devices, window):
        self.sections, self.devices = sections, devices
        self.rows = window
        self.columns = devices // window // CORES
        self.row_groups = [
            [self.index(y, x, c) for y in range(self.rows)]
            for x in range(self.columns)
            for c in range(CORES)
        ]

    def index(self, y, x, c):
        return ((y % self.rows) * self.columns + x % self.columns) * CORES + c % CORES

    def pairs(self, dy, dx, dc):
        return [
            (self.index(y, x, c), self.index(y + dy, x + dx, c + dc))
            for y in range(self.rows)
            for x in range(self.columns)
            for c in range(CORES)
        ]

    def move(self, array, dy=0, dx=0, dc=0):
        return lax.ppermute(array, "expert", self.pairs(dy, dx, dc))

    def relay(self, array, by, dy=0):
        if dy == 0:
            pairs = [(s, (s + by) % self.sections) for s in range(self.sections)]
            return lax.ppermute(array, "section", pairs)
        pairs = [
            (s * self.devices + i, ((s + by) % self.sections) * self.devices + j)
            for s in range(self.sections)
            for i, j in self.pairs(dy, 0, 0)
        ]
        return lax.ppermute(array, ("section", "expert"), pairs)

    def exchange(self, array):
        blocks = array.reshape(self.rows, -1, array.shape[-1])
        out = lax.all_to_all(
            blocks, "expert", 0, 0, tiled=True, axis_index_groups=self.row_groups
        )
        return out.reshape(array.shape)

    def near(self, mine):
        return self.move(mine, dx=1), self.move(mine, dx=-1)

    def far(self, left, right):
        middle = left.shape[0] // 2
        return self.move(left[:middle], dx=1), self.move(right[middle:], dx=-1)

    def swap(self, arrays):
        return [self.move(a, dc=1) for a in arrays]

    def collect(self, own, other):
        total = own.astype(f32) + other.astype(f32)
        rows = own.shape[0] // 4
        mine, left, right, far = [total[i * rows : (i + 1) * rows] for i in range(4)]
        middle = rows // 2
        far = far.astype(bf16)
        to_right = self.move(far[:middle], dx=1).astype(f32)
        to_left = self.move(far[middle:], dx=-1).astype(f32)
        right = jnp.concatenate([right[:middle] + to_right, right[middle:]], axis=0)
        left = jnp.concatenate([left[:middle], left[middle:] + to_left], axis=0)
        from_left = self.move(right.astype(bf16), dx=1).astype(f32)
        from_right = self.move(left.astype(bf16), dx=-1).astype(f32)
        return (mine + from_left + from_right).astype(bf16)


def block_of(array, index, rows, count=1):
    return lax.dynamic_slice_in_dim(array, index * rows, rows * count, axis=0)


def per_device(
    fwd_input,
    saved_input,
    out_cotangent,
    fwd_routes,
    bwd_routes,
    fwd_scores,
    bwd_scores,
    norm_gain,
    gate_proj,
    up_proj,
    down_proj,
):
    devices = lax.axis_size("expert")
    window = devices // GROUP
    net = Net(lax.axis_size("section"), devices, window)
    gate, up, down = gate_proj[0, 0], up_proj[0, 0], down_proj[0, 0]
    gain = norm_gain
    x_f, x_b, cot = fwd_input[0], saved_input[0], out_cotangent[0]
    routes_f, routes_b = fwd_routes[0].T, bwd_routes[0].T
    scores_f, scores_b = fwd_scores[0].T, bwd_scores[0].T
    width = x_f.shape[1]
    middle = x_f.shape[0] // 2
    row = lax.axis_index("expert") // GROUP
    cb, xs, cs, first, table, weights, inverse = prep_bwd(
        routes_b, scores_b, x_b, cot, gain, window
    )
    rows_f, mixing = prep_fwd(routes_f, scores_f, x_f, gain, window)

    mine_b = net.exchange(cb).reshape(window, 2, CAP, width)
    mine_b = mine_b.transpose(1, 0, 2, 3).reshape(cb.shape)
    mine_b, rows_f = lax.optimization_barrier((mine_b, rows_f))

    left_b, right_b = net.near(mine_b)
    mine_f = net.exchange(rows_f)
    early_f = net.relay(x_f, 1)
    top_c = net.relay(cot[:middle], -1)
    mixing = block_of(jnp.concatenate([mixing, mixing], axis=0), row, CAP, window)
    mixing = net.relay(mixing, 1)
    left_b, right_b, mine_f, early_f, top_c, mixing = lax.optimization_barrier(
        (left_b, right_b, mine_f, early_f, top_c, mixing)
    )

    far_b = net.far(left_b, right_b)
    near_f = net.near(mine_f)
    near_b = [mine_b, left_b, right_b]
    near_b = near_b + net.swap(near_b)
    bottom_c = net.relay(after(cot, near_b[5])[middle:], -1)
    near_h = enter_bwd([(a, 0) for a in near_b], [(a, 1) for a in near_b], gate, up, down)
    far_b, near_f, near_h, bottom_c = lax.optimization_barrier((far_b, near_f, near_h, bottom_c))

    far_f = net.far(*near_f)
    far_b = [*far_b, *net.swap(far_b)]
    far_h = enter_bwd([(a, 0) for a in far_b[0::2]], [(a, 0) for a in far_b[1::2]], gate, up, down)
    own, peer = leave_bwd(near_h, far_h, gate, up)
    other = net.move(peer, dc=1)
    own, other, far_f = lax.optimization_barrier((own, other, far_f))

    dn = net.exchange(net.collect(own, other))
    own_f = [mine_f, *near_f, *far_f]
    own, peer = expert_fwd(own_f, net.swap(own_f), gate, up, down)
    outs = net.collect(own, net.move(peer, dc=1))
    outs = [
        net.relay(block_of(outs, lax.rem(row + window - d, window), CAP), 1, dy=-d)
        for d in range(window)
    ]
    grads, score_rows = grad_slots(
        routes_b, scores_b, table, first, weights, inverse, xs, cs, gain, dn
    )
    late_b = net.relay(grads, -1)
    fwd_handoff = place(place_fwd_kernel, "place_fwd", mixing, (early_f,), *outs)
    grad_handoff = place_grad((top_c, bottom_c), late_b)
    return (fwd_handoff[None], grad_handoff[None], score_rows.T[None])


def solution(mesh):
    tokens = P("section", "expert", None)
    slices = P("section", "expert", None, None)
    in_specs = (tokens,) * 7 + (P("section", None),) + (slices,) * 3
    return jax.shard_map(
        per_device, mesh=mesh, in_specs=in_specs, out_specs=(tokens,) * 3, check_vma=False
    )
```
